32 devices in a mesh: groups: 2 (over x), gx: 8 (over z, y), gy: 2 (over core).
Axes of the slice: x: 2, y: 2, z: 4, core: 2. Of those that a mesh axis runs over, the one named last changes fastest.
Arguments:
- inputs: bfloat16 [1024, 8192], P(('groups', 'gx'), 'gy'), parts along dimension 0, may hold values from -6 to 6
- out_grad: bfloat16 [1024, 8192], P(('groups', 'gx'), 'gy'), parts along dimension 0, may hold values from -1.5 to 1.5
- w_gate: bfloat16 [8192, 14336], P('gy', 'gx'), may hold values from -0.0625 to 0.0625
- w_up: bfloat16 [8192, 14336], P('gy', 'gx'), may hold values from -0.0625 to 0.0625
- w_down: bfloat16 [14336, 8192], P('gx', 'gy'), may hold values from -0.046875 to 0.046875
Outputs:
- input_grad: bfloat16 [1024, 8192], P(('groups', 'gx'), 'gy'), parts along dimension 0
- gate_wgrad: bfloat16 [16384, 14336], P(('groups', 'gy'), 'gx'), parts along dimension 0
- up_wgrad: bfloat16 [16384, 14336], P(('groups', 'gy'), 'gx'), parts along dimension 0
- down_wgrad: bfloat16 [28672, 8192], P(('groups', 'gx'), 'gy'), parts along dimension 0
The draws below stay inside these ranges and needn't reach their ends.
There are 2 independent parts, one for each index of `groups`. The reference program is written for one: setup_inputs(seed, part) draws one part's arguments, and reference() takes and returns one part's arrays. A program takes and returns all parts, laid end to end along the dimension named above; an argument that names none is the same for every part. Nothing has to cross between parts.
All inputs are finite; a program needn't handle non-finite values.
Results may differ from the reference program's by a relative error of at most 0.005.
Values may be sent and summed in bfloat16 or wider, within the bound.
No kernel may reach another device: no remote copies, remote signals or barrier semaphores. Data moves between devices by JAX's collectives and lax.ppermute only.
A program may use at most 256 MiB of HBM per device.

```python
import jax
import jax.numpy as jnp
from jax import lax

D = 8192
FF = 14336
TOKENS = 512


def steps_of(rng, dims, split, smallest, high):
    def one(dim, shards_of):
        steps = jax.random.uniform(jax.random.fold_in(jax.random.fold_in(rng, 6), dim), (shards_of,), jnp.float32, smallest / len(split), high / len(split))
        return jnp.repeat(jnp.exp(steps), dims[dim] // shards_of).reshape((-1,) + (1,) * (len(dims) - dim - 1))

    gain = one(*split[0])
    for cut in split[1:]:
        gain = gain * one(*cut)
    return gain


def scatter_about(key, extent, scale, bound, shards=(), kind=jnp.bfloat16):
    array = scale * jax.random.normal(key, extent, jnp.float32)
    if shards:
        array = array * steps_of(key, extent, shards, -0.22, 0.18)
    return jnp.clip(array, -bound, bound).astype(kind)


def setup_inputs(seed: int = 0, part: int = 0) -> dict:
    arg_keys = jax.random.split(jax.random.key(seed), 6)
    part_keys = jax.random.split(jax.random.fold_in(arg_keys[5], part), 6)
    return {
        "inputs": scatter_about(part_keys[0], (TOKENS, D), 1.0, 6.0, ((0, 8), (1, 2))),
        "out_grad": scatter_about(part_keys[1], (TOKENS, D), 0.25, 1.5, ((0, 8), (1, 2))),
        "w_gate": scatter_about(arg_keys[2], (D, FF), D ** -0.5, 0.0625, ((0, 2), (1, 8))),
        "w_up": scatter_about(arg_keys[3], (D, FF), D ** -0.5, 0.0625, ((0, 2), (1, 8))),
        "w_down": scatter_about(arg_keys[4], (FF, D), FF ** -0.5, 0.046875, ((0, 8), (1, 2))),
    }


def reference(inputs, out_grad, w_gate, w_up, w_down):
    gate_pre = jnp.dot(inputs, w_gate, preferred_element_type=jnp.float32)
    up_pre = jnp.dot(inputs, w_up, preferred_element_type=jnp.float32)
    hidden_grad = lax.dot_general(out_grad, w_down, (((1,), (1,)), ((), ())), preferred_element_type=jnp.float32)
    sig = jax.nn.sigmoid(gate_pre)
    silu_val = gate_pre * sig
    hidden = (silu_val * up_pre).astype(jnp.bfloat16)
    gate_back = (hidden_grad * up_pre * sig * (1.0 + gate_pre * (1.0 - sig))).astype(jnp.bfloat16)
    up_back = (hidden_grad * silu_val).astype(jnp.bfloat16)
    down_wgrad = lax.dot_general(hidden, out_grad, (((0,), (0,)), ((), ())), preferred_element_type=jnp.float32).astype(jnp.bfloat16)
    gate_wgrad = lax.dot_general(inputs, gate_back, (((0,), (0,)), ((), ())), preferred_element_type=jnp.float32).astype(jnp.bfloat16)
    up_wgrad = lax.dot_general(inputs, up_back, (((0,), (0,)), ((), ())), preferred_element_type=jnp.float32).astype(jnp.bfloat16)
    input_grad = lax.dot_general(gate_back, w_gate, (((1,), (1,)), ((), ())), preferred_element_type=jnp.float32)
    input_grad = input_grad + lax.dot_general(up_back, w_up, (((1,), (1,)), ((), ())), preferred_element_type=jnp.float32)
    return input_grad.astype(jnp.bfloat16), gate_wgrad, up_wgrad, down_wgrad
```

```python
import jax
import jax.numpy as jnp
from jax import lax
from jax.experimental import pallas as pl
from jax.experimental.pallas import tpu as pltpu
from jax.sharding import PartitionSpec as P

BF = jnp.bfloat16
F32 = jnp.float32
VMEM_LIMIT = 58 * 2**20
NN = (((1,), (0,)), ((), ()))
NT = (((1,), (1,)), ((), ()))
TN = (((0,), (0,)), ((), ()))


def dot(a, b, dims):
    return lax.dot_general(a, b, dims, preferred_element_type=F32)


def tile_of(extent, wanted):
    for tile in range(wanted, 127, -128):
        if extent % tile == 0:
            return tile
    return extent


def call(kernel, name, flops, nbytes, **kwargs):
    return pl.pallas_call(
        kernel,
        name=name,
        compiler_params=pltpu.CompilerParams(vmem_limit_bytes=VMEM_LIMIT),
        cost_estimate=pl.CostEstimate(flops=flops, bytes_accessed=nbytes, transcendentals=0),
        **kwargs,
    )


def gather_matmul(pieces, weight, dims, name):
    rows, depth = pieces[0].shape
    count = len(pieces)
    tokens = rows * count
    width = weight.shape[1] if dims == NN else weight.shape[0]
    tile = tile_of(width, 256)

    def kernel(*refs):
        piece_refs = refs[:count]
        w_ref, x_ref, own_ref, send_ref, sems = refs[count:]

        @pl.when(pl.program_id(0) == 0)
        def _():
            copies = [
                pltpu.make_async_copy(p, x_ref.at[pl.ds(i * rows, rows)], sems.at[i])
                for i, p in enumerate(piece_refs)
            ]
            for c in copies:
                c.start()
            for c in copies:
                c.wait()

        out = dot(x_ref[...], w_ref[...], dims)
        own_ref[...] = out
        send_ref[...] = out.astype(BF)

    w_spec = (
        pl.BlockSpec((depth, tile), lambda j: (0, j))
        if dims == NN
        else pl.BlockSpec((tile, depth), lambda j: (j, 0))
    )
    return call(
        kernel,
        name,
        2 * tokens * depth * width,
        2 * depth * width,
        grid=(width // tile,),
        in_specs=[pl.BlockSpec(memory_space=pl.ANY)] * count + [w_spec],
        out_specs=[
            pl.BlockSpec((tokens, depth), lambda j: (0, 0)),
            pl.BlockSpec((tokens, tile), lambda j: (0, j)),
            pl.BlockSpec((tokens, tile), lambda j: (0, j)),
        ],
        out_shape=[
            jax.ShapeDtypeStruct((tokens, depth), BF),
            jax.ShapeDtypeStruct((tokens, width), F32),
            jax.ShapeDtypeStruct((tokens, width), BF),
        ],
        scratch_shapes=[pltpu.SemaphoreType.DMA((count,))],
    )(*pieces, weight)


def matmul(x, weight, name):
    tokens, depth = x.shape
    width = weight.shape[1]
    tile = tile_of(width, 256)

    def kernel(x_ref, w_ref, own_ref, send_ref):
        out = dot(x_ref[...], w_ref[...], NN)
        own_ref[...] = out
        send_ref[...] = out.astype(BF)

    return call(
        kernel,
        name,
        2 * tokens * depth * width,
        2 * depth * width,
        grid=(width // tile,),
        in_specs=[
            pl.BlockSpec((tokens, depth), lambda j: (0, 0)),
            pl.BlockSpec((depth, tile), lambda j: (0, j)),
        ],
        out_specs=[pl.BlockSpec((tokens, tile), lambda j: (0, j))] * 2,
        out_shape=[
            jax.ShapeDtypeStruct((tokens, width), F32),
            jax.ShapeDtypeStruct((tokens, width), BF),
        ],
    )(x, weight)


def backward(pre, w_gate, w_up, chunk, chunks, rows, name):
    tokens, width = pre[0].shape
    depth = w_gate.shape[0]
    part = tokens // chunks
    blocks = part // rows
    tile = tile_of(depth, 512)

    def kernel(*refs):
        g_own, g_recv, u_own, u_recv, h_own, h_recv, wg_ref, wu_ref = refs[:8]
        block_refs = refs[8 : 8 + blocks]
        hidden_ref, gb_ref, ub_ref = refs[8 + blocks :]

        @pl.when(pl.program_id(0) == 0)
        def _():
            step = tile_of(width, 256)

            @pl.loop(0, width // step)
            def _(i):
                at = (slice(None), pl.ds(pl.multiple_of(i * step, step), step))
                gate_pre = g_own[at] + g_recv[at].astype(F32)
                up_pre = u_own[at] + u_recv[at].astype(F32)
                hidden_grad = h_own[at] + h_recv[at].astype(F32)
                sig = jax.nn.sigmoid(gate_pre)
                silu_val = gate_pre * sig
                hidden_ref[at] = (silu_val * up_pre).astype(BF)
                gb_ref[at] = (hidden_grad * up_pre * sig * (1.0 + gate_pre * (1.0 - sig))).astype(BF)
                ub_ref[at] = (hidden_grad * silu_val).astype(BF)

        out = dot(gb_ref[...], wg_ref[...], NT) + dot(ub_ref[...], wu_ref[...], NT)
        for i, ref in enumerate(block_refs):
            ref[...] = out[i * rows : (i + 1) * rows].astype(BF)

    whole = pl.BlockSpec((part, width), lambda j: (chunk, 0))
    return call(
        kernel,
        name,
        4 * part * depth * width,
        4 * depth * width,
        grid=(depth // tile,),
        in_specs=[whole] * 6 + [pl.BlockSpec((tile, width), lambda j: (j, 0))] * 2,
        out_specs=[pl.BlockSpec((rows, tile), lambda j: (0, j))] * blocks
        + [pl.BlockSpec((part, width), lambda j: (0, 0))] * 3,
        out_shape=[jax.ShapeDtypeStruct((rows, depth), BF)] * blocks
        + [jax.ShapeDtypeStruct((part, width), BF)] * 3,
    )(*pre, w_gate, w_up)


def weight_grads(x, chunks_of, name):
    tokens, depth = x.shape
    count = len(chunks_of)
    pieces = len(chunks_of[0])
    part, width = chunks_of[0][0].shape
    tile = tile_of(depth, 512)

    def kernel(*refs):
        x_ref = refs[0]
        y_refs = refs[1 : 1 + count * pieces]
        out_refs = refs[1 + count * pieces : 1 + count * pieces + count]
        ys = refs[1 + count * pieces + count : -1]
        sems = refs[-1]

        @pl.when(pl.program_id(0) == 0)
        def _():
            copies = [
                pltpu.make_async_copy(
                    y_refs[k * pieces + i], ys[k].at[pl.ds(i * part, part)], sems.at[k * pieces + i]
                )
                for k in range(count)
                for i in range(pieces)
            ]
            for c in copies:
                c.start()
            for c in copies:
                c.wait()

        for y, out_ref in zip(ys, out_refs):
            out_ref[...] = dot(x_ref[...], y[...], TN).astype(BF)

    return call(
        kernel,
        name,
        2 * tokens * depth * width * count,
        2 * depth * width * count,
        grid=(depth // tile,),
        in_specs=[pl.BlockSpec((tokens, tile), lambda j: (0, j))]
        + [pl.BlockSpec(memory_space=pl.ANY)] * (count * pieces),
        out_specs=[pl.BlockSpec((tile, width), lambda j: (j, 0))] * count,
        out_shape=[jax.ShapeDtypeStruct((depth, width), BF)] * count,
        scratch_shapes=[pltpu.VMEM((tokens, width), BF)] * count
        + [pltpu.SemaphoreType.DMA((count * pieces,))],
    )(x, *[y for ys in chunks_of for y in ys])


def down_grads(hidden_chunks, grad, name):
    tokens, depth = grad.shape
    pieces = len(hidden_chunks)
    part, width = hidden_chunks[0].shape
    tile = tile_of(width, 256)

    def kernel(*refs):
        h_refs, g_ref, out_ref = refs[:pieces], refs[pieces], refs[pieces + 1]
        hidden = jnp.concatenate([h[...] for h in h_refs], axis=0)
        out_ref[...] = dot(hidden, g_ref[...], TN).astype(BF)

    return call(
        kernel,
        name,
        2 * tokens * depth * width,
        2 * depth * width,
        grid=(width // tile,),
        in_specs=[pl.BlockSpec((part, tile), lambda j: (0, j))] * pieces
        + [pl.BlockSpec((tokens, depth), lambda j: (0, 0))],
        out_specs=pl.BlockSpec((tile, depth), lambda j: (j, 0)),
        out_shape=jax.ShapeDtypeStruct((width, depth), BF),
    )(*hidden_chunks, grad)


def ring_body(n, inputs, out_grad, w_gate, w_up, w_down):
    ring = n // 2
    along = [(2 * p + s, 2 * ((p + 1) % ring) + s) for p in range(ring) for s in range(2)]
    across = [(i, i ^ 1) for i in range(n)]
    rows = inputs.shape[0]

    def step(x):
        return lax.ppermute(x, "gx", along)

    def swap(x):
        return lax.ppermute(x, "gx", across)

    def other_core(x):
        return lax.ppermute(x, "gy", [(0, 1), (1, 0)])

    def gather(x):
        mine, theirs = [x], [swap(x)]
        for _ in range(ring - 1):
            mine.append(step(mine[-1]))
            theirs.append(swap(mine[-1]))
        order = list(range(1, ring)) + [0]
        return [b for k in order for b in (mine[k], theirs[k])]

    in_blocks = gather(inputs)
    grad_blocks = gather(out_grad)
    x, gate_own, gate_send = gather_matmul(in_blocks, w_gate, NN, "gate")
    gate_recv = other_core(gate_send)
    up_own, up_send = matmul(x, w_up, "up")
    up_recv = other_core(up_send)
    grad, back_own, back_send = gather_matmul(grad_blocks, w_down, NT, "hidden_grad")
    back_recv = other_core(back_send)
    pre = (gate_own, gate_recv, up_own, up_recv, back_own, back_recv)
    chunks = 2 if ring % 2 == 0 else 1
    blocks, saved = [], []
    for c in range(chunks):
        out = backward(pre, w_gate, w_up, c, chunks, rows, f"back{c}")
        blocks += out[:-3]
        saved.append(out[-3:])
    hidden, gate_back, up_back = zip(*saved)

    total = None
    for k in range(ring):
        part = blocks[2 * k].astype(F32) + swap(blocks[2 * k + 1]).astype(F32)
        if total is not None:
            part = part + total.astype(F32)
        total = part.astype(BF)
        if k < ring - 1:
            total = step(total)
    gate_wgrad, up_wgrad = weight_grads(x, (gate_back, up_back), "in_wgrads")
    down_wgrad = down_grads(hidden, grad, "down_wgrad")
    return (total, gate_wgrad, up_wgrad, down_wgrad)


def swiglu_back(gate_pre, up_pre, hidden_grad):
    sig = jax.nn.sigmoid(gate_pre)
    silu_val = gate_pre * sig
    hidden = (silu_val * up_pre).astype(BF)
    gate_back = (hidden_grad * up_pre * sig * (1.0 + gate_pre * (1.0 - sig))).astype(BF)
    up_back = (hidden_grad * silu_val).astype(BF)
    return (hidden, gate_back, up_back)


def plain_body(inputs, out_grad, w_gate, w_up, w_down):
    gathered_in = lax.all_gather(inputs, "gx", axis=0, tiled=True)
    gathered_grad = lax.all_gather(out_grad, "gx", axis=0, tiled=True)
    parts = (dot(gathered_in, w_gate, NN), dot(gathered_in, w_up, NN), dot(gathered_grad, w_down, NT))
    hidden, gate_back, up_back = swiglu_back(*lax.psum(parts, "gy"))
    down_wgrad = dot(hidden, gathered_grad, TN).astype(BF)
    gate_wgrad = dot(gathered_in, gate_back, TN).astype(BF)
    up_wgrad = dot(gathered_in, up_back, TN).astype(BF)
    result = dot(gate_back, w_gate, NT) + dot(up_back, w_up, NT)
    summed = lax.psum_scatter(result, "gx", scatter_dimension=0, tiled=True)
    return (summed.astype(BF), gate_wgrad, up_wgrad, down_wgrad)


def solution(mesh):
    n = mesh.shape["gx"]

    def body(inputs, out_grad, w_gate, w_up, w_down):
        args = (inputs, out_grad, w_gate, w_up, w_down)
        if n % 2 == 0 and n > 2 and mesh.shape["gy"] == 2 and inputs.shape[0] % 16 == 0:
            return ring_body(n, *args)
        return plain_body(*args)

    in_specs = (
        P(("groups", "gx"), "gy"),
        P(("groups", "gx"), "gy"),
        P("gy", "gx"),
        P("gy", "gx"),
        P("gx", "gy"),
    )
    out_specs = (
        P(("groups", "gx"), "gy"),
        P(("groups", "gy"), "gx"),
        P(("groups", "gy"), "gx"),
        P(("groups", "gx"), "gy"),
    )
    return jax.shard_map(body, mesh=mesh, in_specs=in_specs, out_specs=out_specs, check_vma=False)
```

```python
import jax
import jax.numpy as jnp
from jax import lax
from jax.experimental import pallas as pl
from jax.experimental.pallas import tpu as pltpu
from jax.sharding import PartitionSpec as P

BF = jnp.bfloat16
F32 = jnp.float32
ANY_SPEC = pl.BlockSpec(memory_space=pl.ANY)
HBM_SPEC = pl.BlockSpec(memory_space=pltpu.HBM)
VMEM_SPEC = pl.BlockSpec(memory_space=pltpu.VMEM)
NN = (((1,), (0,)), ((), ()))
NT = (((1,), (1,)), ((), ()))
TN = (((0,), (0,)), ((), ()))


def dot(a, b, dims):
    return lax.dot_general(a, b, dims, preferred_element_type=F32)


def tile_of(extent, wanted):
    for tile in range(wanted, 127, -128):
        if extent % tile == 0:
            return tile
    return extent


def call(kernel, name, flops, nbytes, vmem, **kwargs):
    return pl.pallas_call(
        kernel,
        name=name,
        compiler_params=pltpu.CompilerParams(vmem_limit_bytes=vmem * 2**20),
        cost_estimate=pl.CostEstimate(flops=flops, bytes_accessed=nbytes, transcendentals=0),
        **kwargs,
    )


def run_copies(copies):
    for c in copies:
        c.start()
    for c in copies:
        c.wait()


def in_hbm(x):
    return pltpu.with_memory_space_constraint(x, pltpu.HBM)


def hold(weight, vmem, name):
    def kernel(w_ref, out_ref, sem):
        run_copies([pltpu.make_async_copy(w_ref, out_ref, sem)])

    return call(
        kernel,
        name,
        0,
        2 * weight.size,
        vmem,
        in_specs=[HBM_SPEC],
        out_specs=VMEM_SPEC,
        out_shape=pltpu.VMEM(weight.shape, BF),
        scratch_shapes=[pltpu.SemaphoreType.DMA],
    )(in_hbm(weight))


def gather_matmul(pieces, weights, dims, send_type, name):
    rows, depth = pieces[0].shape
    count, nw = len(pieces), len(weights)
    tokens = rows * count
    width = weights[0].shape[1] if dims == NN else weights[0].shape[0]
    tile = tile_of(width, 256)
    outs = 1 if send_type == F32 else 2

    def kernel(*refs):
        piece_refs, w_refs = refs[:count], refs[count : count + nw]
        x_ref, *out_refs = refs[count + nw : -1]
        sems = refs[-1]

        @pl.when(pl.program_id(0) == 0)
        def _():
            run_copies(
                [
                    pltpu.make_async_copy(p, x_ref.at[pl.ds(i * rows, rows)], sems.at[i])
                    for i, p in enumerate(piece_refs)
                ]
            )

        at = pl.ds(pl.multiple_of(pl.program_id(0) * tile, tile), tile)
        for i, w_ref in enumerate(w_refs):
            out = dot(x_ref[...], w_ref[:, at] if dims == NN else w_ref[at, :], dims)
            for ref in out_refs:
                ref[i] = out.astype(ref.dtype)

    return call(
        kernel,
        name,
        2 * tokens * depth * width * nw,
        2 * tokens * depth,
        17,
        grid=(width // tile,),
        in_specs=[ANY_SPEC] * count + [VMEM_SPEC] * nw,
        out_specs=[pl.BlockSpec((tokens, depth), lambda j: (0, 0))]
        + [pl.BlockSpec((nw, tokens, tile), lambda j: (0, 0, j))] * outs,
        out_shape=[pltpu.HBM((tokens, depth), BF)]
        + [pltpu.HBM((nw, tokens, width), t) for t in (F32, send_type)[:outs]],
        scratch_shapes=[pltpu.SemaphoreType.DMA((count,))],
    )(*pieces, *weights)


def backward(own_gu, recv_gu, own_h, recv_h, w_gate, w_up, rows, name):
    _, tokens, width = own_gu.shape
    depth = w_gate.shape[0]
    blocks = tokens // rows
    act_tile = tile_of(width, 896)
    tile = tile_of(depth, 512)
    act_steps = width // act_tile

    def kernel(*refs):
        own_gu_ref, recv_gu_ref, own_h_ref, recv_h_ref, wg_ref, wu_ref = refs[:6]
        block_refs = refs[6 : 6 + blocks]
        hidden_ref, gb_ref, ub_ref, gb_t, ub_t = refs[6 + blocks :]
        step = pl.program_id(0)

        @pl.when(step < act_steps)
        def _():
            part = tile_of(act_tile, 256)

            @pl.loop(0, act_tile // part)
            def _(i):
                at = pl.ds(pl.multiple_of(i * part, part), part)
                gate_pre = own_gu_ref[0, :, at] + recv_gu_ref[0, :, at].astype(F32)
                up_pre = own_gu_ref[1, :, at] + recv_gu_ref[1, :, at].astype(F32)
                hidden_grad = own_h_ref[0, :, at] + recv_h_ref[0, :, at].astype(F32)
                sig = jax.nn.sigmoid(gate_pre)
                silu_val = gate_pre * sig
                hidden_ref[:, at] = (silu_val * up_pre).astype(BF)
                gate_back = (hidden_grad * up_pre * sig * (1.0 + gate_pre * (1.0 - sig))).astype(BF)
                up_back = (hidden_grad * silu_val).astype(BF)
                gb_ref[:, at] = gate_back
                ub_ref[:, at] = up_back
                lines = pl.ds(pl.multiple_of(step * act_tile + i * part, part), part)
                gb_t[lines, :] = gate_back.T
                ub_t[lines, :] = up_back.T

        @pl.when(step >= act_steps)
        def _():
            at = pl.ds(pl.multiple_of((step - act_steps) * tile, tile), tile)
            out = (dot(wg_ref[at, :], gb_t[...], NN) + dot(wu_ref[at, :], ub_t[...], NN)).T
            for i, ref in enumerate(block_refs):
                ref[...] = out[i * rows : (i + 1) * rows].astype(BF)

    def act_spec(lead):
        return pl.BlockSpec((lead, tokens, act_tile), lambda j: (0, 0, jnp.minimum(j, act_steps - 1)))

    act_out = pl.BlockSpec((tokens, act_tile), lambda j: (0, jnp.minimum(j, act_steps - 1)))
    return call(
        kernel,
        name,
        4 * tokens * depth * width,
        20 * tokens * width,
        31,
        grid=(act_steps + depth // tile,),
        in_specs=[act_spec(2), act_spec(2), act_spec(1), act_spec(1), VMEM_SPEC, VMEM_SPEC],
        out_specs=[pl.BlockSpec((rows, tile), lambda j: (0, jnp.maximum(j - act_steps, 0)))] * blocks + [act_out] * 3,
        out_shape=[pltpu.HBM((rows, depth), BF)] * blocks + [pltpu.HBM((tokens, width), BF)] * 3,
        scratch_shapes=[pltpu.VMEM((width, tokens), BF)] * 2,
    )(in_hbm(own_gu), recv_gu, in_hbm(own_h), recv_h, w_gate, w_up)


def weight_grads(x_chunks, ys_chunks, wanted, name):
    pieces, count = len(x_chunks), len(ys_chunks)
    part, depth = x_chunks[0].shape
    width = ys_chunks[0][0].shape[1]
    tokens = part * pieces
    tile = tile_of(depth, wanted)

    def kernel(*refs):
        x_refs, y_refs = refs[:pieces], refs[pieces : pieces * (1 + count)]
        out_refs = refs[pieces * (1 + count) : pieces * (1 + count) + count]
        ys, sems = refs[-1 - count : -1], refs[-1]

        @pl.when(pl.program_id(0) == 0)
        def _():
            run_copies(
                [
                    pltpu.make_async_copy(
                        y_refs[k * pieces + i], ys[k].at[pl.ds(i * part, part)], sems.at[k * pieces + i]
                    )
                    for k in range(count)
                    for i in range(pieces)
                ]
            )

        x = jnp.concatenate([r[...] for r in x_refs], axis=0)
        for y, out_ref in zip(ys, out_refs):
            out_ref[...] = dot(x, y[...], TN).astype(BF)

    return call(
        kernel,
        name,
        2 * tokens * depth * width * count,
        2 * depth * width * count,
        28,
        grid=(depth // tile,),
        in_specs=[pl.BlockSpec((part, tile), lambda j: (0, j))] * pieces + [ANY_SPEC] * (pieces * count),
        out_specs=[pl.BlockSpec((tile, width), lambda j: (j, 0))] * count,
        out_shape=[pltpu.HBM((depth, width), BF)] * count,
        scratch_shapes=[pltpu.VMEM((tokens, width), BF)] * count + [pltpu.SemaphoreType.DMA((count * pieces,))],
    )(*x_chunks, *[y for ys in ys_chunks for y in ys])


def in_order(*arrays):
    return lax.optimization_barrier(arrays)


def gather_stages(ring):
    along = [f"in {k}" for k in range(1, ring)] + [f"grad {k}" for k in range(1, ring)] + [f"grad other {ring - 1}"]
    across = [f"in other {k}" for k in range(ring)] + [f"grad other {k}" for k in range(1, ring - 1)] + ["grad other 0"]
    kernels = [["gate"], ["up"]] + [[]] * (ring - 3) + [["a"], ["b"], ["down"]]
    kernels += [[]] * (len(along) - 1 - len(kernels)) + [["h_a"]]
    return [([m, s], k) for m, s, k in zip(along, across, kernels)]


def ring_body(n, inputs, out_grad, w_gate, w_up, w_down):
    ring = n // 2
    half = ring // 2
    last = ring - 1
    across = [(i, i ^ 1) for i in range(n)]
    rows = inputs.shape[0]

    def shift(x, by=1):
        pairs = [(2 * p + s, 2 * ((p + by) % ring) + s) for p in range(ring) for s in range(2)]
        return lax.ppermute(x, "gx", pairs)

    def swap(x):
        return lax.ppermute(x, "gx", across)

    def other_core(x):
        return lax.ppermute(x, "gy", [(0, 1), (1, 0)])

    order = list(range(1, ring)) + [0]
    early, late = order[:half], order[half:]
    have = {"in 0": inputs, "grad 0": out_grad, "w_gate": w_gate, "w_up": w_up, "w_down": w_down}

    def blocks_of(name, ks):
        return [b for k in ks for b in (have[f"{name} {k}"], have[f"{name} other {k}"])]

    def source(move):
        name, *other, k = move.split()
        k = int(k)
        if other and (name, k) != ("grad", last):
            return f"{name} {k}", swap
        return " ".join([name, *other, str(k - 1)]), shift

    def products(name, ks, weights, dims, tag):
        out = gather_matmul(blocks_of(name, ks), [have[w] for w in weights], dims, BF, tag)
        return dict(zip((f"{tag} x", f"{tag} own", f"{tag} send"), out))

    def gate_up(ks, tag):
        return lambda: products("in", ks, ("gate", "up"), NN, tag)

    kernels = {
        "gate": lambda: {"gate": hold(have["w_gate"], 45, "hold_gate")},
        "up": lambda: {"up": hold(have["w_up"], 31, "hold_up")},
        "down": lambda: {"down": hold(have["w_down"], 17, "hold_down")},
        "a": gate_up(early, "gu_a"),
        "b": gate_up(late, "gu_b"),
        "h_a": lambda: products("grad", early, ("down",), NT, "h_a"),
    }
    for moves, names in gather_stages(ring):
        fresh = {}
        for move in moves:
            name, how = source(move)
            fresh[move] = how(have[name])
        for name in names:
            fresh.update(kernels[name]())
        have.update(fresh)
        have = dict(zip(have, in_order(*have.values())))

    made = {"w_gate": have["gate"], "w_up": have["up"], "x_a": have["gu_a x"], "x_b": have["gu_b x"]}
    made.update(gu_a=have["gu_a own"], gu_b=have["gu_b own"], gu_send_a=have["gu_a send"], gu_send_b=have["gu_b send"])
    made.update(grad_a=have["h_a x"], h_a=have["h_a own"], h_send_a=have["h_a send"])

    gu_recv_a, gu_recv_b = other_core(made["gu_send_a"]), other_core(made["gu_send_b"])
    h_recv_a = other_core(made["h_send_a"])
    out = products("grad", late, ("down",), NT, "h_b").values()
    grad_b, h_b, h_send_b, h_a = in_order(*out, made["h_a"])
    h_recv_b = other_core(h_send_b)

    weights = (made["w_gate"], made["w_up"])
    out_a = backward(made["gu_a"], gu_recv_a, h_a, h_recv_a, *weights, rows, "back_a")
    *out_a, h_b = in_order(*out_a, h_b)
    own, sent, recv = {}, {}, {}
    for i, k in enumerate(order[:half]):
        own[k], sent[k] = out_a[2 * i : 2 * i + 2]
    for k in reversed(order[:half]):
        recv[k] = swap(sent[k])
    saved_a = out_a[-3:]
    out_b = backward(made["gu_b"], gu_recv_b, h_b, h_recv_b, *weights, rows, "back_b")
    recv[half], *out_b = in_order(recv[half], *out_b)
    for i, k in enumerate(order[half:]):
        own[k], sent[k] = out_b[2 * i : 2 * i + 2]
    saved_b = out_b[-3:]
    hidden, gate_back, up_back = zip(saved_a, saved_b)

    def add(k, *terms):
        total = own[k].astype(F32) + recv[k].astype(F32)
        for t in terms:
            total = total + t.astype(F32)
        return total.astype(BF)

    down = shift(add(half), -1)
    for k in order[half:]:
        if k:
            recv[k] = swap(sent[k])
    (down_wgrad,) = weight_grads(hidden, ((made["grad_a"], grad_b),), 256, "down_wgrad")
    out = in_order(down, recv[half - 1], recv[half + 1], sent[0], down_wgrad)
    down, recv[half - 1], recv[half + 1], sent[0], down_wgrad = out
    for k in range(half - 1, 0, -1):
        down = shift(add(k, down), -1)
    ahead = shift(add(half + 1))
    for k in range(half + 2, ring):
        ahead = shift(add(k, ahead))
    recv[0] = swap(sent[0])
    gate_wgrad, up_wgrad = weight_grads((made["x_a"], made["x_b"]), (gate_back, up_back), 512, "in_wgrads")
    input_grad = add(0, down, ahead)
    return (input_grad, gate_wgrad, up_wgrad, down_wgrad)


def swiglu_back(gate_pre, up_pre, hidden_grad):
    sig = jax.nn.sigmoid(gate_pre)
    silu_val = gate_pre * sig
    hidden = (silu_val * up_pre).astype(BF)
    gate_back = (hidden_grad * up_pre * sig * (1.0 + gate_pre * (1.0 - sig))).astype(BF)
    up_back = (hidden_grad * silu_val).astype(BF)
    return (hidden, gate_back, up_back)


def plain_body(inputs, out_grad, w_gate, w_up, w_down):
    gathered_in = lax.all_gather(inputs, "gx", axis=0, tiled=True)
    gathered_grad = lax.all_gather(out_grad, "gx", axis=0, tiled=True)
    parts = (dot(gathered_in, w_gate, NN), dot(gathered_in, w_up, NN), dot(gathered_grad, w_down, NT))
    hidden, gate_back, up_back = swiglu_back(*lax.psum(parts, "gy"))
    down_wgrad = dot(hidden, gathered_grad, TN).astype(BF)
    gate_wgrad = dot(gathered_in, gate_back, TN).astype(BF)
    up_wgrad = dot(gathered_in, up_back, TN).astype(BF)
    result = dot(gate_back, w_gate, NT) + dot(up_back, w_up, NT)
    summed = lax.psum_scatter(result, "gx", scatter_dimension=0, tiled=True)
    return (summed.astype(BF), gate_wgrad, up_wgrad, down_wgrad)


def solution(mesh):
    n = mesh.shape["gx"]

    def body(inputs, out_grad, w_gate, w_up, w_down):
        args = (inputs, out_grad, w_gate, w_up, w_down)
        if n % 4 == 0 and n >= 8 and mesh.shape["gy"] == 2 and inputs.shape[0] % 16 == 0:
            return ring_body(n, *args)
        return plain_body(*args)

    in_specs = (
        P(("groups", "gx"), "gy"),
        P(("groups", "gx"), "gy"),
        P("gy", "gx"),
        P("gy", "gx"),
        P("gx", "gy"),
    )
    out_specs = (
        P(("groups", "gx"), "gy"),
        P(("groups", "gy"), "gx"),
        P(("groups", "gy"), "gx"),
        P(("groups", "gx"), "gy"),
    )
    return jax.shard_map(body, mesh=mesh, in_specs=in_specs, out_specs=out_specs, check_vma=False)
```

```python
import jax
import jax.numpy as jnp
from jax import lax
from jax.experimental import pallas as pl
from jax.experimental.pallas import tpu as pltpu
from jax.sharding import PartitionSpec as P

BF = jnp.bfloat16
F32 = jnp.float32
ANY_SPEC = pl.BlockSpec(memory_space=pl.ANY)
HBM_SPEC = pl.BlockSpec(memory_space=pltpu.HBM)
VMEM_SPEC = pl.BlockSpec(memory_space=pltpu.VMEM)
NN = (((1,), (0,)), ((), ()))
NT = (((1,), (1,)), ((), ()))
TN = (((0,), (0,)), ((), ()))


def dot(a, b, dims):
    return lax.dot_general(a, b, dims, preferred_element_type=F32)


def tile_of(extent, wanted):
    for tile in range(wanted, 127, -128):
        if extent % tile == 0:
            return tile
    return extent


def call(kernel, name, flops, nbytes, vmem, **kwargs):
    return pl.pallas_call(
        kernel,
        name=name,
        compiler_params=pltpu.CompilerParams(vmem_limit_bytes=vmem * 2**20),
        cost_estimate=pl.CostEstimate(flops=flops, bytes_accessed=nbytes, transcendentals=0),
        **kwargs,
    )


def run_copies(copies):
    for c in copies:
        c.start()
    for c in copies:
        c.wait()


def in_hbm(x):
    return pltpu.with_memory_space_constraint(x, pltpu.HBM)


def hold(weight, vmem, name):
    def kernel(w_ref, out_ref, sem):
        run_copies([pltpu.make_async_copy(w_ref, out_ref, sem)])

    return call(
        kernel,
        name,
        1500 * weight.size,
        4 * weight.size,
        vmem,
        in_specs=[HBM_SPEC],
        out_specs=VMEM_SPEC,
        out_shape=pltpu.VMEM(weight.shape, BF),
        scratch_shapes=[pltpu.SemaphoreType.DMA],
    )(in_hbm(weight))


def gather_matmul(pieces, weights, dims, send_type, name):
    rows, depth = pieces[0].shape
    count, nw = len(pieces), len(weights)
    tokens = rows * count
    width = weights[0].shape[1] if dims == NN else weights[0].shape[0]
    tile = tile_of(width, 256)
    outs = 1 if send_type == F32 else 2

    def kernel(*refs):
        piece_refs, w_refs = refs[:count], refs[count : count + nw]
        x_ref, *out_refs = refs[count + nw : -1]
        sems = refs[-1]

        @pl.when(pl.program_id(0) == 0)
        def _():
            run_copies(
                [
                    pltpu.make_async_copy(p, x_ref.at[pl.ds(i * rows, rows)], sems.at[i])
                    for i, p in enumerate(piece_refs)
                ]
            )

        at = pl.ds(pl.multiple_of(pl.program_id(0) * tile, tile), tile)
        for i, w_ref in enumerate(w_refs):
            out = dot(x_ref[...], w_ref[:, at] if dims == NN else w_ref[at, :], dims)
            for ref in out_refs:
                ref[i] = out.astype(ref.dtype)

    return call(
        kernel,
        name,
        2 * tokens * depth * width * nw,
        2 * tokens * depth,
        17,
        grid=(width // tile,),
        in_specs=[ANY_SPEC] * count + [VMEM_SPEC] * nw,
        out_specs=[pl.BlockSpec((tokens, depth), lambda j: (0, 0))]
        + [pl.BlockSpec((nw, tokens, tile), lambda j: (0, 0, j))] * outs,
        out_shape=[pltpu.HBM((tokens, depth), BF)]
        + [pltpu.HBM((nw, tokens, width), t) for t in (F32, send_type)[:outs]],
        scratch_shapes=[pltpu.SemaphoreType.DMA((count,))],
    )(*pieces, *weights)


def backward(own_gu, recv_gu, own_h, recv_h, w_gate, w_up, rows, name):
    _, tokens, width = own_gu.shape
    depth = w_gate.shape[0]
    blocks = tokens // rows
    act_tile = tile_of(width, 896)
    tile = tile_of(depth, 512)
    act_steps = width // act_tile

    def kernel(*refs):
        own_gu_ref, recv_gu_ref, own_h_ref, recv_h_ref, wg_ref, wu_ref = refs[:6]
        block_refs = refs[6 : 6 + blocks]
        hidden_ref, gb_ref, ub_ref, gb_t, ub_t = refs[6 + blocks :]
        step = pl.program_id(0)

        @pl.when(step < act_steps)
        def _():
            part = tile_of(act_tile, 256)

            @pl.loop(0, act_tile // part)
            def _(i):
                at = pl.ds(pl.multiple_of(i * part, part), part)
                gate_pre = own_gu_ref[0, :, at] + recv_gu_ref[0, :, at].astype(F32)
                up_pre = own_gu_ref[1, :, at] + recv_gu_ref[1, :, at].astype(F32)
                hidden_grad = own_h_ref[0, :, at] + recv_h_ref[0, :, at].astype(F32)
                sig = jax.nn.sigmoid(gate_pre)
                silu_val = gate_pre * sig
                hidden_ref[:, at] = (silu_val * up_pre).astype(BF)
                gate_back = (hidden_grad * up_pre * sig * (1.0 + gate_pre * (1.0 - sig))).astype(BF)
                up_back = (hidden_grad * silu_val).astype(BF)
                gb_ref[:, at] = gate_back
                ub_ref[:, at] = up_back
                lines = pl.ds(pl.multiple_of(step * act_tile + i * part, part), part)
                gb_t[lines, :] = gate_back.T
                ub_t[lines, :] = up_back.T

        @pl.when(step >= act_steps)
        def _():
            at = pl.ds(pl.multiple_of((step - act_steps) * tile, tile), tile)
            out = (dot(wg_ref[at, :], gb_t[...], NN) + dot(wu_ref[at, :], ub_t[...], NN)).T
            for i, ref in enumerate(block_refs):
                ref[...] = out[i * rows : (i + 1) * rows].astype(BF)

    def act_spec(lead):
        return pl.BlockSpec((lead, tokens, act_tile), lambda j: (0, 0, jnp.minimum(j, act_steps - 1)))

    act_out = pl.BlockSpec((tokens, act_tile), lambda j: (0, jnp.minimum(j, act_steps - 1)))
    return call(
        kernel,
        name,
        4 * tokens * depth * width,
        20 * tokens * width,
        31,
        grid=(act_steps + depth // tile,),
        in_specs=[act_spec(2), act_spec(2), act_spec(1), act_spec(1), VMEM_SPEC, VMEM_SPEC],
        out_specs=[pl.BlockSpec((rows, tile), lambda j: (0, jnp.maximum(j - act_steps, 0)))] * blocks + [act_out] * 3,
        out_shape=[pltpu.HBM((rows, depth), BF)] * blocks + [pltpu.HBM((tokens, width), BF)] * 3,
        scratch_shapes=[pltpu.VMEM((width, tokens), BF)] * 2,
    )(in_hbm(own_gu), recv_gu, in_hbm(own_h), recv_h, w_gate, w_up)


def weight_grads(x_chunks, ys_chunks, wanted, name):
    pieces, count = len(x_chunks), len(ys_chunks)
    part, depth = x_chunks[0].shape
    width = ys_chunks[0][0].shape[1]
    tokens = part * pieces
    tile = tile_of(depth, wanted)

    def kernel(*refs):
        x_refs, y_refs = refs[:pieces], refs[pieces : pieces * (1 + count)]
        out_refs = refs[pieces * (1 + count) : pieces * (1 + count) + count]
        ys, sems = refs[-1 - count : -1], refs[-1]

        @pl.when(pl.program_id(0) == 0)
        def _():
            run_copies(
                [
                    pltpu.make_async_copy(
                        y_refs[k * pieces + i], ys[k].at[pl.ds(i * part, part)], sems.at[k * pieces + i]
                    )
                    for k in range(count)
                    for i in range(pieces)
                ]
            )

        x = jnp.concatenate([r[...] for r in x_refs], axis=0)
        for y, out_ref in zip(ys, out_refs):
            out_ref[...] = dot(x, y[...], TN).astype(BF)

    return call(
        kernel,
        name,
        2 * tokens * depth * width * count,
        2 * depth * width * count,
        28,
        grid=(depth // tile,),
        in_specs=[pl.BlockSpec((part, tile), lambda j: (0, j))] * pieces + [ANY_SPEC] * (pieces * count),
        out_specs=[pl.BlockSpec((tile, width), lambda j: (j, 0))] * count,
        out_shape=[pltpu.HBM((depth, width), BF)] * count,
        scratch_shapes=[pltpu.VMEM((tokens, width), BF)] * count + [pltpu.SemaphoreType.DMA((count * pieces,))],
    )(*x_chunks, *[y for ys in ys_chunks for y in ys])


def in_order(*arrays):
    return lax.optimization_barrier(arrays)


STAGES = [
    (["in 1", "in other 0", "in 3", "grad other 0"], ["gate"], ["in 1", "in other 0"]),
    (["in 2", "in other 1"], ["up"], ["in 2", "in other 1", "in 3", "grad other 0"]),
    (["in other 3", "grad 3", "in other 2", "grad 1"], ["down"], ["in other 3", "grad 3"]),
    (["grad other 3"], ["gu_b"], ["in other 2", "grad 1"]),
    (["grad 2", "grad other 1"], ["gu_a"], ["grad other 3", "grad 2"]),
    (["grad other 2"], ["h_b"], ["grad other 2", "grad other 1"]),
]


def ring_body(n, inputs, out_grad, w_gate, w_up, w_down):
    ring = n // 2
    across = [(i, i ^ 1) for i in range(n)]
    rows = inputs.shape[0]

    def shift(x, by=1):
        pairs = [(2 * p + s, 2 * ((p + by) % ring) + s) for p in range(ring) for s in range(2)]
        return lax.ppermute(x, "gx", pairs)

    def swap(x):
        return lax.ppermute(x, "gx", across)

    def other_core(x):
        return lax.ppermute(x, "gy", [(0, 1), (1, 0)])

    early, late = (1, 2), (3, 0)
    have = {"in 0": inputs, "grad 0": out_grad, "w_gate": w_gate, "w_up": w_up, "w_down": w_down}

    def source(move):
        name, *other, k = move.split()
        if other and move != "grad other 1":
            return f"{name} {k}", swap
        by = -1 if k == "3" else 1
        return " ".join([name, *other, str((int(k) - by) % ring)]), lambda x: shift(x, by)

    def products(name, ks, weights, dims, tag):
        blocks = [have[f"{name} {side}{k}"] for k in ks for side in ("", "other ")]
        out = gather_matmul(blocks, [have[w] for w in weights], dims, BF, tag)
        return dict(zip((f"{tag} x", f"{tag} own", f"{tag} send"), out))

    kernels = {
        "gate": lambda: {"gate": hold(have["w_gate"], 45, "hold_gate")},
        "up": lambda: {"up": hold(have["w_up"], 31, "hold_up")},
        "down": lambda: {"down": hold(have["w_down"], 17, "hold_down")},
        "gu_a": lambda: products("in", early, ("gate", "up"), NN, "gu_a"),
        "gu_b": lambda: products("in", late, ("gate", "up"), NN, "gu_b"),
        "h_a": lambda: products("grad", early, ("down",), NT, "h_a"),
        "h_b": lambda: products("grad", late, ("down",), NT, "h_b"),
    }
    moving = {}
    for starts, names, ends in STAGES:
        for move in starts:
            name, how = source(move)
            moving[move] = how(have[name])
        fresh = {}
        for name in names:
            fresh.update(kernels[name]())
        for move in ends:
            fresh[move] = moving.pop(move)
        have.update(fresh)
        have = dict(zip(have, in_order(*have.values())))

    gu_recv_b, gu_recv_a = other_core(have["gu_b send"]), other_core(have["gu_a send"])
    h_recv_b = other_core(have["h_b send"])
    have.update(kernels["h_a"]())
    have = dict(zip(have, in_order(*have.values())))
    h_recv_a = other_core(have["h_a send"])

    weights = (have["gate"], have["up"])
    own, sent, recv = {}, {}, {}
    out_b = backward(have["gu_b own"], gu_recv_b, have["h_b own"], h_recv_b, *weights, rows, "back_b")
    *out_b, h_own_a = in_order(*out_b, have["h_a own"])
    own[3], sent[3], own[0], sent[0] = out_b[:4]
    recv[3] = swap(sent[3])
    recv[0] = swap(sent[0])
    out_a = backward(have["gu_a own"], gu_recv_a, h_own_a, h_recv_a, *weights, rows, "back_a")
    recv[3], *out_a = in_order(recv[3], *out_a)
    own[1], sent[1], own[2], sent[2] = out_a[:4]
    hidden, gate_back, up_back = zip(out_a[4:], out_b[4:])

    def add(k, *terms):
        total = own[k].astype(F32) + recv[k].astype(F32)
        for t in terms:
            total = total + t.astype(F32)
        return total.astype(BF)

    recv[2] = swap(sent[2])
    ahead = shift(add(3))
    recv[1] = swap(sent[1])
    (down_wgrad,) = weight_grads(hidden, ((have["h_a x"], have["h_b x"]),), 256, "down_wgrad")
    recv[2], down_wgrad, *gate_back = in_order(recv[2], down_wgrad, *gate_back)
    back = shift(add(2), -1)
    x = (have["gu_a x"], have["gu_b x"])
    (gate_wgrad,) = weight_grads(x, (gate_back,), 512, "gate_wgrad")
    back, recv[1], gate_wgrad, *up_back = in_order(back, recv[1], gate_wgrad, *up_back)
    back = shift(add(1, back), -1)
    (up_wgrad,) = weight_grads(x, (up_back,), 512, "up_wgrad")
    input_grad = add(0, back, ahead)
    return (input_grad, gate_wgrad, up_wgrad, down_wgrad)


def swiglu_back(gate_pre, up_pre, hidden_grad):
    sig = jax.nn.sigmoid(gate_pre)
    silu_val = gate_pre * sig
    hidden = (silu_val * up_pre).astype(BF)
    gate_back = (hidden_grad * up_pre * sig * (1.0 + gate_pre * (1.0 - sig))).astype(BF)
    up_back = (hidden_grad * silu_val).astype(BF)
    return (hidden, gate_back, up_back)


def plain_body(inputs, out_grad, w_gate, w_up, w_down):
    gathered_in = lax.all_gather(inputs, "gx", axis=0, tiled=True)
    gathered_grad = lax.all_gather(out_grad, "gx", axis=0, tiled=True)
    parts = (dot(gathered_in, w_gate, NN), dot(gathered_in, w_up, NN), dot(gathered_grad, w_down, NT))
    hidden, gate_back, up_back = swiglu_back(*lax.psum(parts, "gy"))
    down_wgrad = dot(hidden, gathered_grad, TN).astype(BF)
    gate_wgrad = dot(gathered_in, gate_back, TN).astype(BF)
    up_wgrad = dot(gathered_in, up_back, TN).astype(BF)
    result = dot(gate_back, w_gate, NT) + dot(up_back, w_up, NT)
    summed = lax.psum_scatter(result, "gx", scatter_dimension=0, tiled=True)
    return (summed.astype(BF), gate_wgrad, up_wgrad, down_wgrad)


def solution(mesh):
    n = mesh.shape["gx"]

    def body(inputs, out_grad, w_gate, w_up, w_down):
        args = (inputs, out_grad, w_gate, w_up, w_down)
        if n == 8 and mesh.shape["gy"] == 2 and inputs.shape[0] % 16 == 0:
            return ring_body(n, *args)
        return plain_body(*args)

    in_specs = (
        P(("groups", "gx"), "gy"),
        P(("groups", "gx"), "gy"),
        P("gy", "gx"),
        P("gy", "gx"),
        P("gx", "gy"),
    )
    out_specs = (
        P(("groups", "gx"), "gy"),
        P(("groups", "gy"), "gx"),
        P(("groups", "gy"), "gx"),
        P(("groups", "gx"), "gy"),
    )
    return jax.shard_map(body, mesh=mesh, in_specs=in_specs, out_specs=out_specs, check_vma=False)
```

```python
import jax
import jax.numpy as jnp
from jax import lax
from jax.experimental import pallas as pl
from jax.experimental.pallas import tpu as pltpu
from jax.sharding import PartitionSpec as P

BF = jnp.bfloat16
F32 = jnp.float32
ANY_SPEC = pl.BlockSpec(memory_space=pl.ANY)
HBM_SPEC = pl.BlockSpec(memory_space=pltpu.HBM)
VMEM_SPEC = pl.BlockSpec(memory_space=pltpu.VMEM)
NN = (((1,), (0,)), ((), ()))
NT = (((1,), (1,)), ((), ()))
TN = (((0,), (0,)), ((), ()))


def dot(a, b, dims):
    return lax.dot_general(a, b, dims, preferred_element_type=F32)


def tile_of(extent, wanted):
    for tile in range(wanted, 127, -128):
        if extent % tile == 0:
            return tile
    return extent


def call(kernel, name, flops, nbytes, vmem, **kwargs):
    return pl.pallas_call(
        kernel,
        name=name,
        compiler_params=pltpu.CompilerParams(vmem_limit_bytes=vmem * 2**20),
        cost_estimate=pl.CostEstimate(flops=flops, bytes_accessed=nbytes, transcendentals=0),
        **kwargs,
    )


def run_copies(copies):
    for c in copies:
        c.start()
    for c in copies:
        c.wait()


def in_hbm(x):
    return pltpu.with_memory_space_constraint(x, pltpu.HBM)


def hold(weight, vmem, name):
    def kernel(w_ref, out_ref, sem):
        run_copies([pltpu.make_async_copy(w_ref, out_ref, sem)])

    return call(
        kernel,
        name,
        1500 * weight.size,
        4 * weight.size,
        vmem,
        in_specs=[HBM_SPEC],
        out_specs=VMEM_SPEC,
        out_shape=pltpu.VMEM(weight.shape, BF),
        scratch_shapes=[pltpu.SemaphoreType.DMA],
    )(in_hbm(weight))


def gather_matmul(pieces, weights, dims, send_type, name):
    rows, depth = pieces[0].shape
    count, nw = len(pieces), len(weights)
    tokens = rows * count
    width = weights[0].shape[1] if dims == NN else weights[0].shape[0]
    tile = tile_of(width, 256)
    outs = 1 if send_type == F32 else 2

    def kernel(*refs):
        piece_refs, w_refs = refs[:count], refs[count : count + nw]
        x_ref, *out_refs = refs[count + nw : -1]
        sems = refs[-1]

        @pl.when(pl.program_id(0) == 0)
        def _():
            run_copies(
                [
                    pltpu.make_async_copy(p, x_ref.at[pl.ds(i * rows, rows)], sems.at[i])
                    for i, p in enumerate(piece_refs)
                ]
            )

        at = pl.ds(pl.multiple_of(pl.program_id(0) * tile, tile), tile)
        for i, w_ref in enumerate(w_refs):
            out = dot(x_ref[...], w_ref[:, at] if dims == NN else w_ref[at, :], dims)
            for ref in out_refs:
                ref[i] = out.astype(ref.dtype)

    return call(
        kernel,
        name,
        2 * tokens * depth * width * nw,
        2 * tokens * depth,
        17,
        grid=(width // tile,),
        in_specs=[ANY_SPEC] * count + [VMEM_SPEC] * nw,
        out_specs=[pl.BlockSpec((tokens, depth), lambda j: (0, 0))]
        + [pl.BlockSpec((nw, tokens, tile), lambda j: (0, 0, j))] * outs,
        out_shape=[pltpu.HBM((tokens, depth), BF)]
        + [pltpu.HBM((nw, tokens, width), t) for t in (F32, send_type)[:outs]],
        scratch_shapes=[pltpu.SemaphoreType.DMA((count,))],
    )(*pieces, *weights)


def backward(own_gu, recv_gu, own_h, recv_h, w_gate, w_up, rows, name):
    _, tokens, width = own_gu.shape
    depth = w_gate.shape[0]
    blocks = tokens // rows
    act_tile = tile_of(width, 896)
    tile = tile_of(depth, 512)
    act_steps = width // act_tile

    def kernel(*refs):
        own_gu_ref, recv_gu_ref, own_h_ref, recv_h_ref, wg_ref, wu_ref = refs[:6]
        block_refs = refs[6 : 6 + blocks]
        hidden_ref, gb_ref, ub_ref, gb_all, ub_all = refs[6 + blocks :]
        step = pl.program_id(0)

        @pl.when(step < act_steps)
        def _():
            part = tile_of(act_tile, 256)

            @pl.loop(0, act_tile // part)
            def _(i):
                at = pl.ds(pl.multiple_of(i * part, part), part)
                gate_pre = own_gu_ref[0, :, at] + recv_gu_ref[0, :, at].astype(F32)
                up_pre = own_gu_ref[1, :, at] + recv_gu_ref[1, :, at].astype(F32)
                hidden_grad = own_h_ref[0, :, at] + recv_h_ref[0, :, at].astype(F32)
                sig = jax.nn.sigmoid(gate_pre)
                silu_val = gate_pre * sig
                hidden_ref[:, at] = (silu_val * up_pre).astype(BF)
                gate_back = (hidden_grad * up_pre * sig * (1.0 + gate_pre * (1.0 - sig))).astype(BF)
                up_back = (hidden_grad * silu_val).astype(BF)
                gb_ref[:, at] = gate_back
                ub_ref[:, at] = up_back
                cols = pl.ds(pl.multiple_of(step * act_tile + i * part, part), part)
                gb_all[:, cols] = gate_back
                ub_all[:, cols] = up_back

        @pl.when(step >= act_steps)
        def _():
            at = pl.ds(pl.multiple_of((step - act_steps) * tile, tile), tile)
            out = dot(gb_all[...], wg_ref[at, :], NT) + dot(ub_all[...], wu_ref[at, :], NT)
            for i, ref in enumerate(block_refs):
                ref[...] = out[i * rows : (i + 1) * rows].astype(BF)

    def act_spec(lead):
        return pl.BlockSpec((lead, tokens, act_tile), lambda j: (0, 0, jnp.minimum(j, act_steps - 1)))

    act_out = pl.BlockSpec((tokens, act_tile), lambda j: (0, jnp.minimum(j, act_steps - 1)))
    return call(
        kernel,
        name,
        4 * tokens * depth * width,
        20 * tokens * width,
        31,
        grid=(act_steps + depth // tile,),
        in_specs=[act_spec(2), act_spec(2), act_spec(1), act_spec(1), VMEM_SPEC, VMEM_SPEC],
        out_specs=[pl.BlockSpec((rows, tile), lambda j: (0, jnp.maximum(j - act_steps, 0)))] * blocks + [act_out] * 3,
        out_shape=[pltpu.HBM((rows, depth), BF)] * blocks + [pltpu.HBM((tokens, width), BF)] * 3,
        scratch_shapes=[pltpu.VMEM((tokens, width), BF)] * 2,
    )(in_hbm(own_gu), recv_gu, in_hbm(own_h), recv_h, w_gate, w_up)


def weight_grads(x_chunks, ys_chunks, wanted, name):
    pieces, count = len(x_chunks), len(ys_chunks)
    part, depth = x_chunks[0].shape
    width = ys_chunks[0][0].shape[1]
    tokens = part * pieces
    tile = tile_of(depth, wanted)

    def kernel(*refs):
        x_refs, y_refs = refs[:pieces], refs[pieces : pieces * (1 + count)]
        out_refs = refs[pieces * (1 + count) : pieces * (1 + count) + count]
        ys, sems = refs[-1 - count : -1], refs[-1]

        @pl.when(pl.program_id(0) == 0)
        def _():
            run_copies(
                [
                    pltpu.make_async_copy(
                        y_refs[k * pieces + i], ys[k].at[pl.ds(i * part, part)], sems.at[k * pieces + i]
                    )
                    for k in range(count)
                    for i in range(pieces)
                ]
            )

        x = jnp.concatenate([r[...] for r in x_refs], axis=0)
        for y, out_ref in zip(ys, out_refs):
            out_ref[...] = dot(x, y[...], TN).astype(BF)

    return call(
        kernel,
        name,
        2 * tokens * depth * width * count,
        2 * depth * width * count,
        28,
        grid=(depth // tile,),
        in_specs=[pl.BlockSpec((part, tile), lambda j: (0, j))] * pieces + [ANY_SPEC] * (pieces * count),
        out_specs=[pl.BlockSpec((tile, width), lambda j: (j, 0))] * count,
        out_shape=[pltpu.HBM((depth, width), BF)] * count,
        scratch_shapes=[pltpu.VMEM((tokens, width), BF)] * count + [pltpu.SemaphoreType.DMA((count * pieces,))],
    )(*x_chunks, *[y for ys in ys_chunks for y in ys])


def in_order(*arrays):
    return lax.optimization_barrier(arrays)


STAGES = [
    (["in 1", "in other 0", "in 3", "grad other 0"], ["gate"], ["in 1", "in other 0"]),
    (["in 2", "in other 1"], ["up"], ["in 2", "in other 1", "in 3", "grad other 0"]),
    (["in other 3", "grad 3", "in other 2", "grad 1"], ["down"], ["in other 3", "grad 3"]),
    (["grad other 3"], ["gu_b"], ["in other 2", "grad 1"]),
    (["grad 2", "grad other 1"], ["gu_a"], ["grad other 3", "grad 2"]),
    (["grad other 2"], ["h_b"], ["grad other 2", "grad other 1"]),
]


def ring_body(n, inputs, out_grad, w_gate, w_up, w_down):
    ring = n // 2
    across = [(i, i ^ 1) for i in range(n)]
    rows = inputs.shape[0]

    def shift(x, by=1):
        pairs = [(2 * p + s, 2 * ((p + by) % ring) + s) for p in range(ring) for s in range(2)]
        return lax.ppermute(x, "gx", pairs)

    def swap(x):
        return lax.ppermute(x, "gx", across)

    def other_core(x):
        return lax.ppermute(x, "gy", [(0, 1), (1, 0)])

    early, late = (1, 2), (3, 0)
    have = {"in 0": inputs, "grad 0": out_grad, "w_gate": w_gate, "w_up": w_up, "w_down": w_down}

    def source(move):
        name, *other, k = move.split()
        if other and move != "grad other 1":
            return f"{name} {k}", swap
        by = -1 if k == "3" else 1
        return " ".join([name, *other, str((int(k) - by) % ring)]), lambda x: shift(x, by)

    def products(name, ks, weights, dims, tag):
        blocks = [have[f"{name} {side}{k}"] for k in ks for side in ("", "other ")]
        out = gather_matmul(blocks, [have[w] for w in weights], dims, BF, tag)
        return dict(zip((f"{tag} x", f"{tag} own", f"{tag} send"), out))

    kernels = {
        "gate": lambda: {"gate": hold(have["w_gate"], 45, "hold_gate")},
        "up": lambda: {"up": hold(have["w_up"], 31, "hold_up")},
        "down": lambda: {"down": hold(have["w_down"], 17, "hold_down")},
        "gu_a": lambda: products("in", early, ("gate", "up"), NN, "gu_a"),
        "gu_b": lambda: products("in", late, ("gate", "up"), NN, "gu_b"),
        "h_a": lambda: products("grad", early, ("down",), NT, "h_a"),
        "h_b": lambda: products("grad", late, ("down",), NT, "h_b"),
    }
    moving = {}
    for starts, names, ends in STAGES:
        for move in starts:
            name, how = source(move)
            moving[move] = how(have[name])
        fresh = {}
        for name in names:
            fresh.update(kernels[name]())
        for move in ends:
            fresh[move] = moving.pop(move)
        have.update(fresh)
        have = dict(zip(have, in_order(*have.values())))

    gu_recv_b, gu_recv_a = other_core(have["gu_b send"]), other_core(have["gu_a send"])
    h_recv_b = other_core(have["h_b send"])
    have.update(kernels["h_a"]())
    have = dict(zip(have, in_order(*have.values())))
    h_recv_a = other_core(have["h_a send"])

    weights = (have["gate"], have["up"])
    own, sent, recv = {}, {}, {}
    out_b = backward(have["gu_b own"], gu_recv_b, have["h_b own"], h_recv_b, *weights, rows, "back_b")
    *out_b, h_own_a = in_order(*out_b, have["h_a own"])
    own[3], sent[3], own[0], sent[0] = out_b[:4]
    recv[3] = swap(sent[3])
    recv[0] = swap(sent[0])
    out_a = backward(have["gu_a own"], gu_recv_a, h_own_a, h_recv_a, *weights, rows, "back_a")
    recv[3], *out_a = in_order(recv[3], *out_a)
    own[1], sent[1], own[2], sent[2] = out_a[:4]
    hidden, gate_back, up_back = zip(out_a[4:], out_b[4:])

    def add(k, *terms):
        total = own[k].astype(F32) + recv[k].astype(F32)
        for t in terms:
            total = total + t.astype(F32)
        return total.astype(BF)

    recv[2] = swap(sent[2])
    ahead = shift(add(3))
    recv[1] = swap(sent[1])
    (down_wgrad,) = weight_grads(hidden, ((have["h_a x"], have["h_b x"]),), 256, "down_wgrad")
    recv[2], down_wgrad, *gate_back = in_order(recv[2], down_wgrad, *gate_back)
    back = shift(add(2), -1)
    x = (have["gu_a x"], have["gu_b x"])
    (gate_wgrad,) = weight_grads(x, (gate_back,), 512, "gate_wgrad")
    back, recv[1], gate_wgrad, *up_back = in_order(back, recv[1], gate_wgrad, *up_back)
    back = shift(add(1, back), -1)
    (up_wgrad,) = weight_grads(x, (up_back,), 512, "up_wgrad")
    input_grad = add(0, back, ahead)
    return (input_grad, gate_wgrad, up_wgrad, down_wgrad)


def swiglu_back(gate_pre, up_pre, hidden_grad):
    sig = jax.nn.sigmoid(gate_pre)
    silu_val = gate_pre * sig
    hidden = (silu_val * up_pre).astype(BF)
    gate_back = (hidden_grad * up_pre * sig * (1.0 + gate_pre * (1.0 - sig))).astype(BF)
    up_back = (hidden_grad * silu_val).astype(BF)
    return (hidden, gate_back, up_back)


def plain_body(inputs, out_grad, w_gate, w_up, w_down):
    gathered_in = lax.all_gather(inputs, "gx", axis=0, tiled=True)
    gathered_grad = lax.all_gather(out_grad, "gx", axis=0, tiled=True)
    parts = (dot(gathered_in, w_gate, NN), dot(gathered_in, w_up, NN), dot(gathered_grad, w_down, NT))
    hidden, gate_back, up_back = swiglu_back(*lax.psum(parts, "gy"))
    down_wgrad = dot(hidden, gathered_grad, TN).astype(BF)
    gate_wgrad = dot(gathered_in, gate_back, TN).astype(BF)
    up_wgrad = dot(gathered_in, up_back, TN).astype(BF)
    result = dot(gate_back, w_gate, NT) + dot(up_back, w_up, NT)
    summed = lax.psum_scatter(result, "gx", scatter_dimension=0, tiled=True)
    return (summed.astype(BF), gate_wgrad, up_wgrad, down_wgrad)


def solution(mesh):
    n = mesh.shape["gx"]

    def body(inputs, out_grad, w_gate, w_up, w_down):
        args = (inputs, out_grad, w_gate, w_up, w_down)
        if n == 8 and mesh.shape["gy"] == 2 and inputs.shape[0] % 16 == 0:
            return ring_body(n, *args)
        return plain_body(*args)

    in_specs = (
        P(("groups", "gx"), "gy"),
        P(("groups", "gx"), "gy"),
        P("gy", "gx"),
        P("gy", "gx"),
        P("gx", "gy"),
    )
    out_specs = (
        P(("groups", "gx"), "gy"),
        P(("groups", "gy"), "gx"),
        P(("groups", "gy"), "gx"),
        P(("groups", "gx"), "gy"),
    )
    return jax.shard_map(body, mesh=mesh, in_specs=in_specs, out_specs=out_specs, check_vma=False)
```
